128 devices in a mesh: dp: 16 (over y, x), feat: 8 (over z, core).
Axes of the slice: x: 4, y: 4, z: 4, core: 2. Of those that a mesh axis runs over, the one named last changes fastest.
Arguments:
- features: bfloat16 [8192, 8192], P('dp'), may hold values from -64 to 64
- proj_weight: bfloat16 [8192, 2048], P('dp', 'feat'), may hold values from -0.0625 to 0.0625
- partner: int32 [8192], P('dp'), may hold values from 0 to 8191, as said below
Outputs:
- grad_proj: float32 [8192, 2048], P('dp', 'feat')
The draws below stay inside these ranges and needn't reach their ends.
Inputs may be any that keep to these rules, and one draw needn't show every extreme that they name: Pairing is mutual (partner[partner[i]] = i). The rows of each aligned block d of 512 rows are paired, in some order, with the rows of block (d + 8) mod (16).
All inputs are finite; a program needn't handle non-finite values.
Results may differ from the reference program's by a relative error of at most 0.03.
Values may be sent and summed in bfloat16 or wider, within the bound.
No kernel may reach another device: no remote copies, remote signals or barrier semaphores. Data moves between devices by JAX's collectives and lax.ppermute only.
A program may use at most 384 MiB of HBM per device.

```python
import math
import jax
import jax.numpy as jnp
from jax import lax

F = 8192
E = 2048
ROWS = 512
BATCH = 8192


def pair_tables(key):
    half_count = BATCH // ROWS // 2
    sub_keys = jax.random.split(jax.random.fold_in(key, 11), half_count)
    forward = jax.vmap(lambda sub_key: jax.random.permutation(sub_key, ROWS))(sub_keys).astype(jnp.int32)
    backward = jnp.argsort(forward, axis=1, stable=True).astype(jnp.int32)
    return (forward, backward, half_count)


def draw_partner(key, part):
    forward, backward, half_count = pair_tables(key)
    block_ids = jnp.arange(half_count, dtype=jnp.int32)[:, None]
    first_half = (block_ids + half_count) * ROWS + forward
    second_half = block_ids * ROWS + backward
    return jnp.concatenate([first_half, second_half], axis=0).reshape(-1).astype(jnp.int32)


def draw_features(key, part):
    forward, backward, half_count = pair_tables(key)
    base_key = jax.random.fold_in(key, 23)
    noise_key = jax.random.fold_in(key, 29)
    scale_key = jax.random.fold_in(key, 31)
    offset_key = jax.random.fold_in(key, 41)
    base_rows = jax.random.normal(base_key, (half_count, ROWS, F), jnp.float32)
    noise_rows = 0.6 * jax.random.normal(noise_key, (2, half_count, ROWS, F), jnp.float32)
    view_offsets = 0.8 * jax.random.normal(offset_key, (2, F), jnp.float32)
    view_one = base_rows + noise_rows[0] + view_offsets[0][None, None, :]
    view_two = jax.vmap(lambda rows_blk, order_idx: jnp.take(rows_blk, order_idx, axis=0))(base_rows, backward) + noise_rows[1] + view_offsets[1][None, None, :]
    all_rows = jnp.concatenate([view_one, view_two], axis=0).reshape(BATCH, F)
    row_scale = jnp.exp(jax.random.uniform(scale_key, (BATCH, 1), jnp.float32, 0.0, math.log(10.0)))
    return jnp.clip(all_rows * row_scale, -64.0, 64.0).astype(jnp.bfloat16)


def steps_of(own_key, extent, pieces, smallest, largest):
    loudness, own = 1.0, jax.random.fold_in(own_key, 6)
    for dim, parts in pieces:
        steps = jnp.exp(jax.random.uniform(jax.random.fold_in(own, dim), (parts,), jnp.float32, smallest / len(pieces), largest / len(pieces)))
        loudness = loudness * jnp.repeat(steps, extent[dim] // parts).reshape([-1 if axis == dim else 1 for axis in range(len(extent))])
    return loudness


def centred(rng, extent, spread, bound, cuts=(), kind=jnp.bfloat16):
    array = jax.random.normal(rng, extent, jnp.float32) * spread
    if len(cuts) > 0:
        array = steps_of(rng, extent, cuts, -0.22, 0.18) * array
    return jnp.clip(array, min=-bound, max=bound).astype(kind)


def setup_inputs(seed: int = 0) -> dict:
    key_of = jax.random.split(jax.random.key(seed), 4)
    features = draw_features(jax.random.fold_in(key_of[3], 71), 0)
    proj_weight = centred(key_of[1], (F, E), F ** -0.5, 0.0625, ((0, 16), (1, 8)))
    partner = draw_partner(jax.random.fold_in(key_of[3], 71), 0)
    return dict(features=features, proj_weight=proj_weight, partner=partner)


ridge = 0.0001
norm_eps = 1e-06

def reference(features, proj_weight, partner):
    batch_size = features.shape[0]
    emb_width = proj_weight.shape[1]
    highest = lax.Precision.HIGHEST
    projected = jnp.dot(features.astype(jnp.float32), proj_weight.astype(jnp.float32), preferred_element_type=jnp.float32)
    col_mean = lax.optimization_barrier(jnp.sum(projected, axis=0)) / batch_size
    centered = (projected - col_mean).astype(jnp.bfloat16)
    identity = jnp.eye(emb_width, dtype=jnp.float32)
    covariance = jnp.dot(centered.T.astype(jnp.float32), centered.astype(jnp.float32), preferred_element_type=jnp.float32) / batch_size + ridge * identity
    factor = jnp.linalg.cholesky(covariance)
    whitener = lax.linalg.triangular_solve(factor, identity, left_side=True, lower=True)
    whitened = jnp.dot(centered.astype(jnp.float32), whitener.T, precision=highest)
    inv_norm = lax.rsqrt(lax.optimization_barrier(jnp.sum(whitened * whitened, axis=1)) + norm_eps)
    unit_rows = whitened * inv_norm[:, None]
    mate_rows = jnp.take(unit_rows, partner, axis=0)
    pair_diff = unit_rows - mate_rows
    grad_unit = 4.0 / math.sqrt(batch_size) * pair_diff
    row_dots = lax.optimization_barrier(jnp.sum(unit_rows * grad_unit, axis=1))
    grad_white = inv_norm[:, None] * (grad_unit - unit_rows * row_dots[:, None])
    moment = jnp.dot(grad_white.T, whitened, precision=highest)
    lower_part = jnp.tril(moment, -1) + 0.5 * jnp.diag(jnp.diag(moment))
    sym = lower_part + lower_part.T
    back_white = grad_white - jnp.dot(whitened, sym, precision=highest) / batch_size
    back_center = jnp.dot(back_white, whitener, precision=highest)
    back_proj = (back_center - lax.optimization_barrier(jnp.sum(back_center, axis=0)) / batch_size).astype(jnp.bfloat16)
    grad_proj = jnp.dot(features.T.astype(jnp.float32), back_proj.astype(jnp.float32), preferred_element_type=jnp.float32)
    return grad_proj
```

```python
import math

import jax
import jax.numpy as jnp
from jax import lax
from jax.experimental import pallas as pl
from jax.experimental.pallas import tpu as pltpu
from jax.sharding import PartitionSpec as P

ridge = 0.0001
norm_eps = 1e-06
f32 = jnp.float32
bf16 = jnp.bfloat16


def from_behind(array, axis, by):
    peers = lax.axis_size(axis)
    return lax.ppermute(array, axis, [(i, (i + by) % peers) for i in range(peers)])


def split_two(value):
    high = value.astype(bf16)
    return high, (value - high.astype(f32)).astype(bf16)


def mat(left, right):
    return jnp.dot(left, right, preferred_element_type=f32)


def mat_high(left, right):
    return jnp.dot(left, right, preferred_element_type=f32, precision=lax.Precision.HIGHEST)


def invert_small(matrix):
    size = matrix.shape[0]
    groups = size // 8
    lane = lax.broadcasted_iota(jnp.int32, (8, size), 1)
    sub = lax.broadcasted_iota(jnp.int32, (8, size), 0)
    rows = [matrix[8 * i : 8 * i + 8] for i in range(groups)]
    for g in range(groups):
        base = 8 * g
        panel = rows[g]
        inside = (lane >= base) & (lane < base + 8)
        cols = [
            jnp.broadcast_to(panel[:, base + j : base + j + 1], (8, size)) for j in range(8)
        ]
        panel = jnp.where(inside, jnp.where(lane - base == sub, 1.0, 0.0), panel)
        for j in range(8):
            inv = 1.0 / jnp.broadcast_to(cols[j][j : j + 1, :], (8, size))
            here = sub == j
            factor = cols[j] * inv
            pivot_row = jnp.broadcast_to(panel[j : j + 1, :], (8, size))
            for m in range(j + 1, 8):
                entry = jnp.broadcast_to(cols[m][j : j + 1, :], (8, size))
                cols[m] = jnp.where(here, entry * inv, cols[m] - factor * entry)
            panel = jnp.where(here, pivot_row * inv, panel - factor * pivot_row)
        spread = [jnp.broadcast_to(panel[j : j + 1, :], (8, size)) for j in range(8)]
        for i in list(range(g + 1, groups)) + list(range(g)):
            old = rows[i]
            total = jnp.where(inside, 0.0, old)
            for j in range(8):
                total = total - (
                    jnp.broadcast_to(old[:, base + j : base + j + 1], (8, size)) * spread[j]
                )
            rows[i] = total
        rows[g] = panel
    return jnp.concatenate(rows, axis=0)


def invert_panel(block):
    half = block.shape[0] // 2
    b11, b12 = block[:half, :half], block[:half, half:]
    b21, b22 = block[half:, :half], block[half:, half:]
    p1 = invert_small(b11)
    r1 = mat_high(p1, b12)
    low = mat_high(b21, p1)
    p2 = invert_small(b22 - mat_high(b21, r1))
    q = mat_high(r1, p2)
    top = jnp.concatenate([p1 + mat_high(q, low), -q], axis=1)
    bottom = jnp.concatenate([-mat_high(p2, low), p2], axis=1)
    return jnp.concatenate([top, bottom], axis=0)


def inverse_kernel(batch_size, packed, out, work, left, right, fresh):
    pairs, blk, _ = packed.shape
    blocks = 2 * pairs
    size = work.shape[0]
    wide = fresh.shape[0]
    steps = size // wide
    diagonal = lax.broadcasted_iota(jnp.int32, (blk, blk), 0) == lax.broadcasted_iota(
        jnp.int32, (blk, blk), 1
    )
    ridge_tile = jnp.where(diagonal, ridge, 0.0)
    for a in range(blocks):
        for c in range(a + 1):
            if a < pairs:
                tile = packed[a, :, c * blk : (c + 1) * blk]
            else:
                at = (blocks - a + c) * blk
                tile = packed[blocks - 1 - a, :, at : at + blk]
            tile = tile * (1.0 / batch_size)
            if c == a:
                tile = tile + ridge_tile
            work[a * blk : (a + 1) * blk, c * blk : (c + 1) * blk] = tile
            if c != a:
                work[c * blk : (c + 1) * blk, a * blk : (a + 1) * blk] = tile.T

    def step(k, carry):
        at_k = pl.ds(pl.multiple_of(k * wide, wide), wide)
        pivot = invert_panel(work[at_k, at_k])
        pivot_high, pivot_low = split_two(pivot)
        for i in range(steps):
            rows = slice(i * wide, (i + 1) * wide)
            high, low = split_two(work[rows, at_k])
            left[rows, :wide] = high
            left[rows, wide : 2 * wide] = low
            left[rows, 2 * wide :] = high
        for j in range(steps):
            lanes = slice(j * wide, (j + 1) * wide)
            high, low = split_two(work[at_k, lanes])
            fresh[:, lanes] = mat(pivot_high, high) + (
                mat(pivot_high, low) + mat(pivot_low, high)
            )
        fresh[:, at_k] = pivot
        for j in range(steps):
            lanes = slice(j * wide, (j + 1) * wide)
            high, low = split_two(fresh[:, lanes])
            right[:wide, lanes] = high
            right[wide : 2 * wide, lanes] = high
            right[2 * wide :, lanes] = low
        work[:, at_k] = jnp.zeros((size, wide), f32)

        def update(j, inner):
            lanes = pl.ds(pl.multiple_of(j * wide, wide), wide)
            for part in range(2):
                rows = slice(part * size // 2, (part + 1) * size // 2)
                work[rows, lanes] = work[rows, lanes] - mat(left[rows, :], right[:, lanes])
            return inner

        lax.fori_loop(0, steps, update, 0)
        work[at_k, :] = fresh[...]
        return carry

    lax.fori_loop(0, steps, step, 0)
    for i in range(steps):
        rows = slice(i * wide, (i + 1) * wide)
        high, low = split_two(work[rows, :])
        out[0, rows, :] = high
        out[1, rows, :] = low


def inverse_parts(packed, size, batch_size, wide=256):
    return pl.pallas_call(
        lambda *refs: inverse_kernel(batch_size, *refs),
        out_shape=jax.ShapeDtypeStruct((2, size, size), bf16),
        scratch_shapes=[
            pltpu.VMEM((size, size), f32),
            pltpu.VMEM((size, 3 * wide), bf16),
            pltpu.VMEM((3 * wide, size), bf16),
            pltpu.VMEM((wide, size), f32),
        ],
        compiler_params=pltpu.CompilerParams(vmem_limit_bytes=60 * 2**20),
    )(packed)


def sum_shares(array, axis):
    return jnp.sum(
        lax.all_to_all(array, axis, 0, 0, tiled=True).astype(f32), axis=0
    )


def three_parts(vector):
    high = lax.reduce_precision(vector, 8, 7)
    rest = vector - high
    mid = lax.reduce_precision(rest, 8, 7)
    rows = jnp.stack([high, mid, rest - mid]).astype(bf16)
    return jnp.pad(rows, ((0, 13), (0, 0)))


def body(features, proj_weight, partner):
    row_count = features.shape[0]
    feat_count = lax.axis_size("feat")
    dp_count = lax.axis_size("dp")
    own_cols = proj_weight.shape[1]
    emb_width = own_cols * feat_count
    blk_width = emb_width // (2 * feat_count)
    batch_size = row_count * dp_count
    feat_idx = lax.axis_index("feat")
    dp_idx = lax.axis_index("dp")

    def own(matrix, axis=1):
        return lax.dynamic_slice_in_dim(matrix, feat_idx * own_cols, own_cols, axis)

    def pick_cols(matrix, blk_index):
        return lax.dynamic_slice_in_dim(matrix, blk_index * blk_width, blk_width, 1)

    weight = lax.all_gather(proj_weight, "dp", axis=0, tiled=True)
    feature_sum = jnp.sum(features.astype(f32), axis=0)
    feature_sum = jnp.sum(lax.all_gather(feature_sum, "dp"), axis=0)
    col_mean = jnp.sum(mat(three_parts(feature_sum), weight), axis=0) / batch_size
    own_centered = (mat(features, weight) - col_mean).astype(bf16)
    centered = lax.all_gather(own_centered, "feat", axis=1, tiled=True)

    received = from_behind(centered, "dp", dp_count // 2)
    first = mat(pick_cols(centered, feat_idx).T, centered)
    second = mat(pick_cols(centered, 2 * feat_count - 1 - feat_idx).T, centered)
    joined = jnp.concatenate([first, second], axis=1)
    lead_cols = (feat_idx + 1) * blk_width
    shifted = lax.dynamic_slice_in_dim(joined, emb_width - lead_cols, emb_width + blk_width, 1)
    column = lax.broadcasted_iota(jnp.int32, (1, emb_width + blk_width), 1)
    cov_pack = jnp.where(column < lead_cols, joined[:, : emb_width + blk_width], shifted)
    cov_share = sum_shares(
        cov_pack.reshape(dp_count, blk_width // dp_count, emb_width + blk_width), "dp"
    )
    packed = lax.all_gather(cov_share, ("feat", "dp"), axis=0, tiled=True)
    packed = packed.reshape(feat_count, blk_width, emb_width + blk_width)

    local_pos = partner - (dp_idx + dp_count // 2) % dp_count * row_count
    mates = jnp.take(received, local_pos, axis=0)
    center_sum = jnp.sum(centered.astype(f32), axis=0)
    center_sum = jnp.sum(lax.all_gather(center_sum, "dp"), axis=0)
    sum_rows = three_parts(center_sum)
    packed, mates, sum_rows = lax.optimization_barrier((packed, mates, sum_rows))

    parts = inverse_parts(packed, emb_width, batch_size)
    white_rows = mat(centered, parts[0]) + mat(centered, parts[1])
    mate_white = mat(mates, parts[0]) + mat(mates, parts[1])
    sum_white = jnp.sum(mat(sum_rows, parts[0]) + mat(sum_rows, parts[1]), axis=0)
    mates_wide = mates.astype(f32)
    norm_sq = jnp.sum(white_rows * centered.astype(f32), axis=1)
    cross = jnp.sum(white_rows * mates_wide, axis=1)
    mate_sq = jnp.sum(mate_white * mates_wide, axis=1)
    inv_norm = lax.rsqrt(norm_sq + norm_eps)
    mate_inv = lax.rsqrt(mate_sq + norm_eps)
    scale = 4.0 / math.sqrt(batch_size)
    alpha = scale * inv_norm * inv_norm * (
        cross * inv_norm * mate_inv + norm_eps * inv_norm * inv_norm
    )
    beta = -scale * inv_norm * mate_inv
    own_back = alpha[:, None] * own(white_rows) + beta[:, None] * own(mate_white)
    own_sum = jnp.sum(own_back, axis=0)

    moment = mat(centered.T, own_back.astype(bf16)) / batch_size
    shares = moment.reshape(dp_count, emb_width // dp_count, own_cols).astype(bf16)
    sum_high = lax.reduce_precision(own_sum, 8, 7)
    sum_two = jnp.stack([sum_high, own_sum - sum_high]).astype(bf16)
    sum_two = jnp.broadcast_to(jnp.pad(sum_two, ((0, 14), (0, 0))), (dp_count, 16, own_cols))
    reduced = sum_shares(jnp.concatenate([shares, sum_two], axis=1), "dp")
    own_total = reduced[-16] + reduced[-15]
    moment_share = reduced[:-16].astype(bf16)
    moment = lax.all_to_all(
        jnp.broadcast_to(moment_share, (dp_count,) + moment_share.shape), "dp", 0, 0, tiled=True
    ).reshape(emb_width, own_cols)
    back_center = own_back - mat(white_rows.astype(bf16), moment)
    sum_moment = jnp.sum(sum_white[:, None] * moment.astype(f32), axis=0)
    back_mean = (own_total - sum_moment) / batch_size
    back_proj = (back_center - back_mean).astype(bf16)
    grad = mat(features.T, back_proj).astype(bf16)
    return sum_shares(grad.reshape(dp_count, -1, own_cols), "dp")


def solution(mesh):
    return jax.shard_map(
        body,
        mesh=mesh,
        in_specs=(P("dp", None), P("dp", "feat"), P("dp")),
        out_specs=P("dp", "feat"),
        check_vma=False,
    )
```

```python
import math

import jax
import jax.numpy as jnp
from jax import lax
from jax.experimental import pallas as pl
from jax.experimental.pallas import tpu as pltpu
from jax.sharding import PartitionSpec as P

ridge = 0.0001
norm_eps = 1e-06
f32 = jnp.float32
bf16 = jnp.bfloat16


def from_behind(array, axis, by):
    peers = lax.axis_size(axis)
    return lax.ppermute(array, axis, [(i, (i + by) % peers) for i in range(peers)])


def split_two(value):
    high = value.astype(bf16)
    return high, (value - high.astype(f32)).astype(bf16)


def mat(left, right):
    return jnp.dot(left, right, preferred_element_type=f32)


def mat_high(left, right):
    return jnp.dot(left, right, preferred_element_type=f32, precision=lax.Precision.HIGHEST)


def invert_small(matrix, result):
    size = matrix.shape[0]
    groups = size // 8
    lane = lax.broadcasted_iota(jnp.int32, (8, size), 1)
    sub = lax.broadcasted_iota(jnp.int32, (8, size), 0)
    rows = [matrix[8 * i : 8 * i + 8] for i in range(groups)]
    for g in range(groups):
        base = 8 * g
        panel = rows[g]
        inside = (lane >= base) & (lane < base + 8)
        cols = [
            jnp.broadcast_to(panel[:, base + j : base + j + 1], (8, size)) for j in range(8)
        ]
        panel = jnp.where(inside, jnp.where(lane - base == sub, 1.0, 0.0), panel)
        for j in range(8):
            inv = 1.0 / jnp.broadcast_to(cols[j][j : j + 1, :], (8, size))
            here = sub == j
            factor = cols[j] * inv
            pivot_row = jnp.broadcast_to(panel[j : j + 1, :], (8, size))
            for m in range(j + 1, 8):
                entry = jnp.broadcast_to(cols[m][j : j + 1, :], (8, size))
                cols[m] = jnp.where(here, entry * inv, cols[m] - factor * entry)
            panel = jnp.where(here, pivot_row * inv, panel - factor * pivot_row)
        spread = [jnp.broadcast_to(panel[j : j + 1, :], (8, size)) for j in range(8)]
        for i in list(range(g + 1, groups)) + list(range(g)):
            old = rows[i]
            total = jnp.where(inside, 0.0, old)
            for j in range(8):
                total = total - (
                    jnp.broadcast_to(old[:, base + j : base + j + 1], (8, size)) * spread[j]
                )
            rows[i] = total
        rows[g] = panel
        yield
    result.append(jnp.concatenate(rows, axis=0))


def invert_panel(block, result):
    half = block.shape[0] // 2
    b11, b12 = block[:half, :half], block[:half, half:]
    b21, b22 = block[half:, :half], block[half:, half:]
    found = []
    yield from invert_small(b11, found)
    p1 = found.pop()
    r1 = mat_high(p1, b12)
    low = mat_high(b21, p1)
    yield from invert_small(b22 - mat_high(b21, r1), found)
    p2 = found.pop()
    q = mat_high(r1, p2)
    top = jnp.concatenate([p1 + mat_high(q, low), -q], axis=1)
    bottom = jnp.concatenate([-mat_high(p2, low), p2], axis=1)
    result.append(jnp.concatenate([top, bottom], axis=0))


def inverse_kernel(
    batch_size, which, packed, rows_in, rows_out, own_out, work, left, right, fresh, pivots
):
    pairs, blk, _ = packed.shape
    blocks = 2 * pairs
    size = work.shape[0]
    wide = fresh.shape[0]
    steps = size // wide
    diagonal = lax.broadcasted_iota(jnp.int32, (blk, blk), 0) == lax.broadcasted_iota(
        jnp.int32, (blk, blk), 1
    )
    ridge_tile = jnp.where(diagonal, ridge, 0.0)
    for a in range(blocks):
        for c in range(a + 1):
            if a < pairs:
                tile = packed[a, :, c * blk : (c + 1) * blk]
            else:
                at = (blocks - a + c) * blk
                tile = packed[blocks - 1 - a, :, at : at + blk]
            tile = tile * (1.0 / batch_size)
            if c == a:
                tile = tile + ridge_tile
            work[a * blk : (a + 1) * blk, c * blk : (c + 1) * blk] = tile
            if c != a:
                work[c * blk : (c + 1) * blk, a * blk : (a + 1) * blk] = tile.T
    found = []
    for _ in invert_panel(work[:wide, :wide], found):
        pass
    pivots[...] = found.pop()

    def step(k, carry):
        at_k = pl.ds(pl.multiple_of(k * wide, wide), wide)
        pivot = pivots[...]
        pivot_high, pivot_low = split_two(pivot)
        for i in range(steps):
            rows = slice(i * wide, (i + 1) * wide)
            high, low = split_two(work[rows, at_k])
            left[rows, :wide] = high
            left[rows, wide : 2 * wide] = low
            left[rows, 2 * wide :] = high
        for j in range(steps):
            lanes = slice(j * wide, (j + 1) * wide)
            high, low = split_two(work[at_k, lanes])
            fresh[:, lanes] = mat(pivot_high, high) + (
                mat(pivot_high, low) + mat(pivot_low, high)
            )
        fresh[:, at_k] = pivot
        for j in range(steps):
            lanes = slice(j * wide, (j + 1) * wide)
            high, low = split_two(fresh[:, lanes])
            right[:wide, lanes] = high
            right[wide : 2 * wide, lanes] = high
            right[2 * wide :, lanes] = low
        work[:, at_k] = jnp.zeros((size, wide), f32)

        after = pl.ds(pl.multiple_of(jnp.minimum(k + 1, steps - 1) * wide, wide), wide)
        coming = []
        inversion = invert_panel(
            work[after, after] - mat(left[after, :], right[:, after]), coming
        )
        for j in range(steps):
            lanes = slice(j * wide, (j + 1) * wide)
            for part in range(2):
                rows = slice(part * size // 2, (part + 1) * size // 2)
                next(inversion, None)
                next(inversion, None)
                work[rows, lanes] = work[rows, lanes] - mat(left[rows, :], right[:, lanes])
        for _ in inversion:
            pass
        pivots[...] = coming.pop()
        work[at_k, :] = fresh[...]
        return carry

    lax.fori_loop(0, steps, step, 0)

    def apply(j, carry):
        lanes = pl.ds(pl.multiple_of(j * wide, wide), wide)
        high, low = split_two(work[:, lanes])
        rows_out[:, lanes] = mat(rows_in[...], high) + mat(rows_in[...], low)
        return carry

    lax.fori_loop(0, steps, apply, 0)
    own_cols = own_out.shape[2]
    own_lanes = pl.ds(pl.multiple_of(which[0] * own_cols, own_cols), own_cols)
    high, low = split_two(work[:, own_lanes])
    own_out[0] = high
    own_out[1] = low


def apply_inverse(packed, rows, which, own_cols, batch_size, wide=256):
    count, size = rows.shape
    in_vmem = pl.BlockSpec(memory_space=pltpu.VMEM)
    return pl.pallas_call(
        lambda *refs: inverse_kernel(batch_size, *refs),
        out_shape=(
            jax.ShapeDtypeStruct((count, size), f32),
            jax.ShapeDtypeStruct((2, size, own_cols), bf16),
        ),
        in_specs=[pl.BlockSpec(memory_space=pltpu.SMEM), in_vmem, in_vmem],
        out_specs=(in_vmem, in_vmem),
        scratch_shapes=[
            pltpu.VMEM((size, size), f32),
            pltpu.VMEM((size, 3 * wide), bf16),
            pltpu.VMEM((3 * wide, size), bf16),
            pltpu.VMEM((wide, size), f32),
            pltpu.VMEM((wide, wide), f32),
        ],
        compiler_params=pltpu.CompilerParams(vmem_limit_bytes=60 * 2**20),
        cost_estimate=pl.CostEstimate(
            flops=150_000_000_000, bytes_accessed=20_000_000, transcendentals=0
        ),
    )(which, packed, rows)


def sum_shares(array, axis):
    return jnp.sum(
        lax.all_to_all(array, axis, 0, 0, tiled=True).astype(f32), axis=0
    )


def three_parts(vector):
    high = lax.reduce_precision(vector, 8, 7)
    rest = vector - high
    mid = lax.reduce_precision(rest, 8, 7)
    rows = jnp.stack([high, mid, rest - mid]).astype(bf16)
    return jnp.pad(rows, ((0, 13), (0, 0)))


def body(features, proj_weight, partner):
    row_count = features.shape[0]
    feat_count = lax.axis_size("feat")
    dp_count = lax.axis_size("dp")
    own_cols = proj_weight.shape[1]
    emb_width = own_cols * feat_count
    blk_width = emb_width // (2 * feat_count)
    batch_size = row_count * dp_count
    feat_idx = lax.axis_index("feat")
    dp_idx = lax.axis_index("dp")

    def own(matrix, axis=1):
        return lax.dynamic_slice_in_dim(matrix, feat_idx * own_cols, own_cols, axis)

    def pick_cols(matrix, blk_index):
        return lax.dynamic_slice_in_dim(matrix, blk_index * blk_width, blk_width, 1)

    weight = lax.all_gather(proj_weight, "dp", axis=0, tiled=True)
    feature_sum = jnp.sum(features.astype(f32), axis=0)
    feature_sum = jnp.sum(lax.all_gather(feature_sum, "dp"), axis=0)
    col_mean = jnp.sum(mat(three_parts(feature_sum), weight), axis=0) / batch_size
    own_centered = (mat(features, weight) - col_mean).astype(bf16)
    centered = lax.all_gather(own_centered, "feat", axis=1, tiled=True)

    first = mat(pick_cols(centered, feat_idx).T, centered)
    second = mat(pick_cols(centered, 2 * feat_count - 1 - feat_idx).T, centered)
    joined = jnp.concatenate([first, second], axis=1)
    lead_cols = (feat_idx + 1) * blk_width
    shifted = lax.dynamic_slice_in_dim(joined, emb_width - lead_cols, emb_width + blk_width, 1)
    column = lax.broadcasted_iota(jnp.int32, (1, emb_width + blk_width), 1)
    cov_pack = jnp.where(column < lead_cols, joined[:, : emb_width + blk_width], shifted)
    cov_share = sum_shares(
        cov_pack.reshape(dp_count, blk_width // dp_count, emb_width + blk_width), "dp"
    )
    packed = lax.all_gather(cov_share, ("feat", "dp"), axis=0, tiled=True)
    packed = packed.reshape(feat_count, blk_width, emb_width + blk_width)

    center_sum = jnp.sum(centered.astype(f32), axis=0)
    center_sum = jnp.sum(lax.all_gather(center_sum, "dp"), axis=0)
    all_rows = jnp.concatenate([centered, three_parts(center_sum)], axis=0)
    packed, centered, all_rows = lax.optimization_barrier((packed, centered, all_rows))

    received = from_behind(centered, "dp", dp_count // 2)
    white_all, own_inverse = apply_inverse(
        packed, all_rows, feat_idx.reshape(1), own_cols, batch_size
    )
    white_rows = white_all[:row_count]
    sum_white = jnp.sum(white_all[row_count:], axis=0)
    norm_sq = jnp.sum(white_rows * centered.astype(f32), axis=1)
    local_pos = partner - (dp_idx + dp_count // 2) % dp_count * row_count
    chosen = local_pos[:, None] == lax.broadcasted_iota(jnp.int32, (row_count, row_count), 1)
    mates = mat(chosen.astype(bf16), received).astype(bf16)
    mate_sq = jnp.sum(
        jnp.where(chosen, from_behind(norm_sq, "dp", dp_count // 2)[None, :], 0.0), axis=1
    )
    mate_own = mat(mates, own_inverse[0]) + mat(mates, own_inverse[1])
    cross = jnp.sum(white_rows * mates.astype(f32), axis=1)
    inv_norm = lax.rsqrt(norm_sq + norm_eps)
    mate_inv = lax.rsqrt(mate_sq + norm_eps)
    scale = 4.0 / math.sqrt(batch_size)
    alpha = scale * inv_norm * inv_norm * (
        cross * inv_norm * mate_inv + norm_eps * inv_norm * inv_norm
    )
    beta = -scale * inv_norm * mate_inv
    own_back = alpha[:, None] * own(white_rows) + beta[:, None] * mate_own
    own_sum = jnp.sum(own_back, axis=0)

    moment = mat(centered.T, own_back.astype(bf16)) / batch_size
    shares = moment.reshape(dp_count, emb_width // dp_count, own_cols).astype(bf16)
    sum_high = lax.reduce_precision(own_sum, 8, 7)
    sum_two = jnp.stack([sum_high, own_sum - sum_high]).astype(bf16)
    sum_two = jnp.broadcast_to(jnp.pad(sum_two, ((0, 14), (0, 0))), (dp_count, 16, own_cols))
    reduced = sum_shares(jnp.concatenate([shares, sum_two], axis=1), "dp")
    own_total = reduced[-16] + reduced[-15]
    moment_share = reduced[:-16].astype(bf16)
    moment = lax.all_to_all(
        jnp.broadcast_to(moment_share, (dp_count,) + moment_share.shape), "dp", 0, 0, tiled=True
    ).reshape(emb_width, own_cols)
    back_center = own_back - mat(white_rows.astype(bf16), moment)
    sum_moment = jnp.sum(sum_white[:, None] * moment.astype(f32), axis=0)
    back_mean = (own_total - sum_moment) / batch_size
    back_proj = (back_center - back_mean).astype(bf16)
    grad = mat(features.T, back_proj).astype(bf16)
    return sum_shares(grad.reshape(dp_count, -1, own_cols), "dp")


def solution(mesh):
    return jax.shard_map(
        body,
        mesh=mesh,
        in_specs=(P("dp", None), P("dp", "feat"), P("dp")),
        out_specs=P("dp", "feat"),
        check_vma=False,
    )
```

```python
import math

import jax
import jax.numpy as jnp
from jax import lax
from jax.experimental import pallas as pl
from jax.experimental.pallas import tpu as pltpu
from jax.sharding import PartitionSpec as P

ridge = 0.0001
norm_eps = 1e-06
f32 = jnp.float32
bf16 = jnp.bfloat16


def from_behind(array, axis, by):
    peers = lax.axis_size(axis)
    return lax.ppermute(array, axis, [(i, (i + by) % peers) for i in range(peers)])


def split_two(value):
    high = value.astype(bf16)
    return high, (value - high.astype(f32)).astype(bf16)


def mat(left, right):
    return jnp.dot(left, right, preferred_element_type=f32)


def mat_high(left, right):
    return jnp.dot(left, right, preferred_element_type=f32, precision=lax.Precision.HIGHEST)


def invert_small(matrix, result):
    size = matrix.shape[0]
    groups = size // 8
    lane = lax.broadcasted_iota(jnp.int32, (8, size), 1)
    sub = lax.broadcasted_iota(jnp.int32, (8, size), 0)
    rows = [matrix[8 * i : 8 * i + 8] for i in range(groups)]
    for g in range(groups):
        base = 8 * g
        panel = rows[g]
        inside = (lane >= base) & (lane < base + 8)
        cols = [
            jnp.broadcast_to(panel[:, base + j : base + j + 1], (8, size)) for j in range(8)
        ]
        panel = jnp.where(inside, jnp.where(lane - base == sub, 1.0, 0.0), panel)
        for j in range(8):
            inv = 1.0 / jnp.broadcast_to(cols[j][j : j + 1, :], (8, size))
            here = sub == j
            factor = cols[j] * inv
            pivot_row = jnp.broadcast_to(panel[j : j + 1, :], (8, size))
            for m in range(j + 1, 8):
                entry = jnp.broadcast_to(cols[m][j : j + 1, :], (8, size))
                cols[m] = jnp.where(here, entry * inv, cols[m] - factor * entry)
            panel = jnp.where(here, pivot_row * inv, panel - factor * pivot_row)
        spread = [jnp.broadcast_to(panel[j : j + 1, :], (8, size)) for j in range(8)]
        for i in list(range(g + 1, groups)) + list(range(g)):
            old = rows[i]
            total = jnp.where(inside, 0.0, old)
            for j in range(8):
                total = total - (
                    jnp.broadcast_to(old[:, base + j : base + j + 1], (8, size)) * spread[j]
                )
            rows[i] = total
        rows[g] = panel
        yield
    result.append(jnp.concatenate(rows, axis=0))


def invert_panel(block, result):
    half = block.shape[0] // 2
    b11, b12 = block[:half, :half], block[:half, half:]
    b21, b22 = block[half:, :half], block[half:, half:]
    found = []
    yield from invert_small(b11, found)
    p1 = found.pop()
    r1 = mat_high(p1, b12)
    low = mat_high(b21, p1)
    yield from invert_small(b22 - mat_high(b21, r1), found)
    p2 = found.pop()
    q = mat_high(r1, p2)
    top = jnp.concatenate([p1 + mat_high(q, low), -q], axis=1)
    bottom = jnp.concatenate([-mat_high(p2, low), p2], axis=1)
    result.append(jnp.concatenate([top, bottom], axis=0))


def inverse_kernel(
    batch_size, which, packed, rows_in, rows_out, own_out, work, left, right, fresh, pivots
):
    pairs, blk, _ = packed.shape
    blocks = 2 * pairs
    size = work.shape[0]
    wide = fresh.shape[0]
    steps = size // wide
    diagonal = lax.broadcasted_iota(jnp.int32, (blk, blk), 0) == lax.broadcasted_iota(
        jnp.int32, (blk, blk), 1
    )
    ridge_tile = jnp.where(diagonal, ridge, 0.0)

    def unpack(a, c):
        if a < pairs:
            tile = packed[a, :, c * blk : (c + 1) * blk]
        else:
            at = (blocks - a + c) * blk
            tile = packed[blocks - 1 - a, :, at : at + blk]
        tile = tile * (1.0 / batch_size)
        if c == a:
            tile = tile + ridge_tile
        work[a * blk : (a + 1) * blk, c * blk : (c + 1) * blk] = tile
        if c != a:
            work[c * blk : (c + 1) * blk, a * blk : (a + 1) * blk] = tile.T

    tiles = [(a, c) for a in range(blocks) for c in range(a + 1)]
    ahead = (wide // blk) * (wide // blk + 1) // 2
    for a, c in tiles[:ahead]:
        unpack(a, c)
    found = []
    inversion = invert_panel(work[:wide, :wide], found)
    for at, (a, c) in enumerate(tiles[ahead:]):
        if at % 4 == 0:
            next(inversion, None)
        unpack(a, c)
    for _ in inversion:
        pass
    pivots[...] = found.pop()

    def sweep(k, look_ahead):
        at_k = pl.ds(pl.multiple_of(k * wide, wide), wide)
        pivot = pivots[...]
        pivot_high, pivot_low = split_two(pivot)

        def scaled(lanes):
            high, low = split_two(work[at_k, lanes])
            return mat(pivot_high, high) + (mat(pivot_high, low) + mat(pivot_low, high))

        coming = []
        inversion = iter(())
        if look_ahead:
            after = pl.ds(pl.multiple_of((k + 1) * wide, wide), wide)
            row_high, row_low = split_two(scaled(after))
            col_high, col_low = split_two(work[after, at_k])
            change = mat(col_high, row_high) + (mat(col_low, row_high) + mat(col_high, row_low))
            inversion = invert_panel(work[after, after] - change, coming)
        for i in range(steps):
            rows = slice(i * wide, (i + 1) * wide)
            high, low = split_two(work[rows, at_k])
            left[rows, :wide] = high
            left[rows, wide : 2 * wide] = low
            left[rows, 2 * wide :] = high
            if i % 2 == 0:
                next(inversion, None)
        for j in range(steps):
            lanes = slice(j * wide, (j + 1) * wide)
            fresh[:, lanes] = scaled(lanes)
            if j % 2 == 0:
                next(inversion, None)
        fresh[:, at_k] = pivot
        for j in range(steps):
            lanes = slice(j * wide, (j + 1) * wide)
            high, low = split_two(fresh[:, lanes])
            right[:wide, lanes] = high
            right[wide : 2 * wide, lanes] = high
            right[2 * wide :, lanes] = low
            if j % 2 == 0:
                next(inversion, None)
        work[:, at_k] = jnp.zeros((size, wide), f32)
        for j in range(steps):
            lanes = slice(j * wide, (j + 1) * wide)
            for part in range(2):
                rows = slice(part * size // 2, (part + 1) * size // 2)
                next(inversion, None)
                if part:
                    next(inversion, None)
                work[rows, lanes] = work[rows, lanes] - mat(left[rows, :], right[:, lanes])
        for _ in inversion:
            pass
        if look_ahead:
            pivots[...] = coming.pop()
        work[at_k, :] = fresh[...]

    def step(k, carry):
        sweep(k, True)
        return carry

    lax.fori_loop(0, steps - 1, step, 0)
    sweep(steps - 1, False)

    def apply(j, carry):
        lanes = pl.ds(pl.multiple_of(j * wide, wide), wide)
        high, low = split_two(work[:, lanes])
        rows_out[:, lanes] = mat(rows_in[...], high) + mat(rows_in[...], low)
        return carry

    lax.fori_loop(0, steps, apply, 0)
    own_cols = own_out.shape[2]
    own_lanes = pl.ds(pl.multiple_of(which[0] * own_cols, own_cols), own_cols)
    high, low = split_two(work[:, own_lanes])
    own_out[0] = high
    own_out[1] = low


def apply_inverse(packed, rows, which, own_cols, batch_size, wide=256):
    count, size = rows.shape
    in_vmem = pl.BlockSpec(memory_space=pltpu.VMEM)
    return pl.pallas_call(
        lambda *refs: inverse_kernel(batch_size, *refs),
        out_shape=(
            jax.ShapeDtypeStruct((count, size), f32),
            jax.ShapeDtypeStruct((2, size, own_cols), bf16),
        ),
        in_specs=[pl.BlockSpec(memory_space=pltpu.SMEM), in_vmem, in_vmem],
        out_specs=(in_vmem, in_vmem),
        scratch_shapes=[
            pltpu.VMEM((size, size), f32),
            pltpu.VMEM((size, 3 * wide), bf16),
            pltpu.VMEM((3 * wide, size), bf16),
            pltpu.VMEM((wide, size), f32),
            pltpu.VMEM((wide, wide), f32),
        ],
        compiler_params=pltpu.CompilerParams(vmem_limit_bytes=60 * 2**20),
        cost_estimate=pl.CostEstimate(
            flops=150_000_000_000, bytes_accessed=20_000_000, transcendentals=0
        ),
    )(which, packed, rows)


def sum_shares(array, axis):
    return jnp.sum(
        lax.all_to_all(array, axis, 0, 0, tiled=True).astype(f32), axis=0
    )


def three_parts(vector):
    high = lax.reduce_precision(vector, 8, 7)
    rest = vector - high
    mid = lax.reduce_precision(rest, 8, 7)
    rows = jnp.stack([high, mid, rest - mid]).astype(bf16)
    return jnp.pad(rows, ((0, 13), (0, 0)))


def body(features, proj_weight, partner):
    row_count = features.shape[0]
    feat_count = lax.axis_size("feat")
    dp_count = lax.axis_size("dp")
    own_cols = proj_weight.shape[1]
    emb_width = own_cols * feat_count
    blk_width = emb_width // (2 * feat_count)
    batch_size = row_count * dp_count
    feat_idx = lax.axis_index("feat")
    dp_idx = lax.axis_index("dp")

    def own(matrix, axis=1):
        return lax.dynamic_slice_in_dim(matrix, feat_idx * own_cols, own_cols, axis)

    def pick_cols(matrix, blk_index):
        return lax.dynamic_slice_in_dim(matrix, blk_index * blk_width, blk_width, 1)

    weight = lax.all_gather(proj_weight, "dp", axis=0, tiled=True)
    feature_sum = jnp.sum(features.astype(f32), axis=0)
    feature_sum = jnp.sum(lax.all_gather(feature_sum, "dp"), axis=0)
    cuts = 2
    by_owner = features.reshape(row_count, dp_count, cuts, -1)
    turned = [by_owner[:, :, cut].reshape(row_count, -1).T for cut in range(cuts)]
    feature_sum, *turned = lax.optimization_barrier((feature_sum, *turned))
    col_mean = jnp.sum(mat(three_parts(feature_sum), weight), axis=0) / batch_size
    own_centered = (mat(features, weight) - col_mean).astype(bf16)
    centered = lax.all_gather(own_centered, "feat", axis=1, tiled=True)

    first = mat(pick_cols(centered, feat_idx).T, centered)
    second = mat(pick_cols(centered, 2 * feat_count - 1 - feat_idx).T, centered)
    joined = jnp.concatenate([first, second], axis=1)
    lead_cols = (feat_idx + 1) * blk_width
    shifted = lax.dynamic_slice_in_dim(joined, emb_width - lead_cols, emb_width + blk_width, 1)
    column = lax.broadcasted_iota(jnp.int32, (1, emb_width + blk_width), 1)
    cov_pack = jnp.where(column < lead_cols, joined[:, : emb_width + blk_width], shifted)
    cov_share = sum_shares(
        cov_pack.reshape(dp_count, blk_width // dp_count, emb_width + blk_width), "dp"
    )
    packed = lax.all_gather(cov_share, ("feat", "dp"), axis=0, tiled=True)
    packed = packed.reshape(feat_count, blk_width, emb_width + blk_width)

    center_sum = jnp.sum(centered.astype(f32), axis=0)
    center_sum = jnp.sum(lax.all_gather(center_sum, "dp"), axis=0)
    all_rows = jnp.concatenate([centered, three_parts(center_sum)], axis=0)
    packed, centered, all_rows = lax.optimization_barrier((packed, centered, all_rows))

    received = from_behind(centered, "dp", dp_count // 2)
    white_all, own_inverse = apply_inverse(
        packed, all_rows, feat_idx.reshape(1), own_cols, batch_size
    )
    white_rows = white_all[:row_count]
    sum_white = jnp.sum(white_all[row_count:], axis=0)
    norm_sq = jnp.sum(white_rows * centered.astype(f32), axis=1)
    local_pos = partner - (dp_idx + dp_count // 2) % dp_count * row_count
    chosen = local_pos[:, None] == lax.broadcasted_iota(jnp.int32, (row_count, row_count), 1)
    mates = mat(chosen.astype(bf16), received).astype(bf16)
    mate_sq = jnp.sum(
        jnp.where(chosen, from_behind(norm_sq, "dp", dp_count // 2)[None, :], 0.0), axis=1
    )
    mate_own = mat(mates, own_inverse[0]) + mat(mates, own_inverse[1])
    cross = jnp.sum(white_rows * mates.astype(f32), axis=1)
    inv_norm = lax.rsqrt(norm_sq + norm_eps)
    mate_inv = lax.rsqrt(mate_sq + norm_eps)
    scale = 4.0 / math.sqrt(batch_size)
    alpha = scale * inv_norm * inv_norm * (
        cross * inv_norm * mate_inv + norm_eps * inv_norm * inv_norm
    )
    beta = -scale * inv_norm * mate_inv
    own_back = alpha[:, None] * own(white_rows) + beta[:, None] * mate_own
    own_sum = jnp.sum(own_back, axis=0)

    moment = mat(centered.T, own_back.astype(bf16)) / batch_size
    shares = moment.reshape(dp_count, emb_width // dp_count, own_cols).astype(bf16)
    sum_high = lax.reduce_precision(own_sum, 8, 7)
    sum_two = jnp.stack([sum_high, own_sum - sum_high]).astype(bf16)
    sum_two = jnp.broadcast_to(jnp.pad(sum_two, ((0, 14), (0, 0))), (dp_count, 16, own_cols))
    reduced = sum_shares(jnp.concatenate([shares, sum_two], axis=1), "dp")
    own_total = reduced[-16] + reduced[-15]
    moment_share = reduced[:-16].astype(bf16)
    moment = lax.all_to_all(
        jnp.broadcast_to(moment_share, (dp_count,) + moment_share.shape), "dp", 0, 0, tiled=True
    ).reshape(emb_width, own_cols)
    back_center = own_back - mat(white_rows.astype(bf16), moment)
    sum_moment = jnp.sum(sum_white[:, None] * moment.astype(f32), axis=0)
    back_mean = (own_total - sum_moment) / batch_size
    back_proj = (back_center - back_mean).astype(bf16)
    grads = [
        sum_shares(mat(part, back_proj).astype(bf16).reshape(dp_count, -1, own_cols), "dp")
        for part in turned
    ]
    return jnp.concatenate(grads, axis=0)


def solution(mesh):
    return jax.shard_map(
        body,
        mesh=mesh,
        in_specs=(P("dp", None), P("dp", "feat"), P("dp")),
        out_specs=P("dp", "feat"),
        check_vma=False,
    )
```

```python
import math

import jax
import jax.numpy as jnp
from jax import lax
from jax.experimental import pallas as pl
from jax.experimental.pallas import tpu as pltpu
from jax.sharding import PartitionSpec as P

ridge = 0.0001
norm_eps = 1e-06
f32 = jnp.float32
bf16 = jnp.bfloat16


def from_behind(array, axis, by):
    peers = lax.axis_size(axis)
    return lax.ppermute(array, axis, [(i, (i + by) % peers) for i in range(peers)])


def split_two(value):
    high = value.astype(bf16)
    return high, (value - high.astype(f32)).astype(bf16)


def mat(left, right):
    return jnp.dot(left, right, preferred_element_type=f32)


def mat_fine(left, right):
    left_high, left_low = split_two(left)
    right_high, right_low = split_two(right)
    return mat(left_high, right_high) + (mat(left_high, right_low) + mat(left_low, right_high))


def invert_small(matrix, result):
    size = matrix.shape[0]
    groups = size // 8
    lane = lax.broadcasted_iota(jnp.int32, (8, size), 1)
    sub = lax.broadcasted_iota(jnp.int32, (8, size), 0)
    rows = [matrix[8 * i : 8 * i + 8] for i in range(groups)]
    for g in range(groups):
        base = 8 * g
        panel = rows[g]
        inside = (lane >= base) & (lane < base + 8)
        cols = [
            jnp.broadcast_to(panel[:, base + j : base + j + 1], (8, size)) for j in range(8)
        ]
        panel = jnp.where(inside, jnp.where(lane - base == sub, 1.0, 0.0), panel)
        for j in range(8):
            inv = 1.0 / jnp.broadcast_to(cols[j][j : j + 1, :], (8, size))
            here = sub == j
            factor = cols[j] * inv
            pivot_row = jnp.broadcast_to(panel[j : j + 1, :], (8, size))
            for m in range(j + 1, 8):
                entry = jnp.broadcast_to(cols[m][j : j + 1, :], (8, size))
                cols[m] = jnp.where(here, entry * inv, cols[m] - factor * entry)
            panel = jnp.where(here, pivot_row * inv, panel - factor * pivot_row)
        spread = [jnp.broadcast_to(panel[j : j + 1, :], (8, size)) for j in range(8)]
        for i in list(range(g + 1, groups)) + list(range(g)):
            old = rows[i]
            total = jnp.where(inside, 0.0, old)
            for j in range(8):
                total = total - (
                    jnp.broadcast_to(old[:, base + j : base + j + 1], (8, size)) * spread[j]
                )
            rows[i] = total
        rows[g] = panel
        yield
    result.append(jnp.concatenate(rows, axis=0))


def invert_panel(block, result):
    half = block.shape[0] // 2
    b11, b12 = block[:half, :half], block[:half, half:]
    b21, b22 = block[half:, :half], block[half:, half:]
    found = []
    yield from invert_small(b11, found)
    p1 = found.pop()
    r1 = mat_fine(p1, b12)
    low = mat_fine(b21, p1)
    yield from invert_small(b22 - mat_fine(b21, r1), found)
    p2 = found.pop()
    q = mat_fine(r1, p2)
    top = jnp.concatenate([p1 + mat_fine(q, low), -q], axis=1)
    bottom = jnp.concatenate([-mat_fine(p2, low), p2], axis=1)
    result.append(jnp.concatenate([top, bottom], axis=0))


def inverse_kernel(
    batch_size, which, packed, rows_in, rows_out, own_out, work, left, right, fresh, pivots
):
    pairs, blk, _ = packed.shape
    blocks = 2 * pairs
    size = work.shape[0]
    wide = fresh.shape[0]
    steps = size // wide
    diagonal = lax.broadcasted_iota(jnp.int32, (blk, blk), 0) == lax.broadcasted_iota(
        jnp.int32, (blk, blk), 1
    )
    ridge_tile = jnp.where(diagonal, ridge, 0.0)

    def unpack(a, c):
        if a < pairs:
            tile = packed[a, :, c * blk : (c + 1) * blk]
        else:
            at = (blocks - a + c) * blk
            tile = packed[blocks - 1 - a, :, at : at + blk]
        tile = tile * (1.0 / batch_size)
        if c == a:
            tile = tile + ridge_tile
        work[a * blk : (a + 1) * blk, c * blk : (c + 1) * blk] = tile
        if c != a:
            work[c * blk : (c + 1) * blk, a * blk : (a + 1) * blk] = tile.T

    tiles = [(a, c) for a in range(blocks) for c in range(a + 1)]
    ahead = (wide // blk) * (wide // blk + 1) // 2
    for a, c in tiles[:ahead]:
        unpack(a, c)
    found = []
    inversion = invert_panel(work[:wide, :wide], found)
    for at, (a, c) in enumerate(tiles[ahead:]):
        if at % 4 == 0:
            next(inversion, None)
        unpack(a, c)
    for _ in inversion:
        pass
    pivots[...] = found.pop()

    def sweep(k, look_ahead):
        at_k = pl.ds(pl.multiple_of(k * wide, wide), wide)
        pivot = pivots[...]
        pivot_high, pivot_low = split_two(pivot)

        def scaled(lanes):
            high, low = split_two(work[at_k, lanes])
            return mat(pivot_high, high) + (mat(pivot_high, low) + mat(pivot_low, high))

        coming = []
        inversion = iter(())
        if look_ahead:
            after = pl.ds(pl.multiple_of((k + 1) * wide, wide), wide)
            row_high, row_low = split_two(scaled(after))
            col_high, col_low = split_two(work[after, at_k])
            change = mat(col_high, row_high) + (mat(col_low, row_high) + mat(col_high, row_low))
            inversion = invert_panel(work[after, after] - change, coming)
        for i in range(steps):
            rows = slice(i * wide, (i + 1) * wide)
            high, low = split_two(work[rows, at_k])
            left[rows, :wide] = high
            left[rows, wide : 2 * wide] = low
            left[rows, 2 * wide :] = high
            if i % 2 == 0:
                next(inversion, None)
        for j in range(steps):
            lanes = slice(j * wide, (j + 1) * wide)
            fresh[:, lanes] = scaled(lanes)
            if j % 2 == 0:
                next(inversion, None)
        fresh[:, at_k] = pivot
        for j in range(steps):
            lanes = slice(j * wide, (j + 1) * wide)
            high, low = split_two(fresh[:, lanes])
            right[:wide, lanes] = high
            right[wide : 2 * wide, lanes] = high
            right[2 * wide :, lanes] = low
            if j % 2 == 0:
                next(inversion, None)
        work[:, at_k] = jnp.zeros((size, wide), f32)
        for j in range(steps):
            lanes = slice(j * wide, (j + 1) * wide)
            for part in range(2):
                rows = slice(part * size // 2, (part + 1) * size // 2)
                next(inversion, None)
                if part:
                    next(inversion, None)
                work[rows, lanes] = work[rows, lanes] - mat(left[rows, :], right[:, lanes])
        for _ in inversion:
            pass
        if look_ahead:
            pivots[...] = coming.pop()
        work[at_k, :] = fresh[...]

    def step(k, carry):
        sweep(k, True)
        return carry

    lax.fori_loop(0, steps - 1, step, 0)
    sweep(steps - 1, False)

    def apply(j, carry):
        lanes = pl.ds(pl.multiple_of(j * wide, wide), wide)
        high, low = split_two(work[:, lanes])
        rows_out[:, lanes] = mat(rows_in[...], high) + mat(rows_in[...], low)
        return carry

    lax.fori_loop(0, steps, apply, 0)
    own_cols = own_out.shape[2]
    own_lanes = pl.ds(pl.multiple_of(which[0] * own_cols, own_cols), own_cols)
    high, low = split_two(work[:, own_lanes])
    own_out[0] = high
    own_out[1] = low


def apply_inverse(packed, rows, which, own_cols, batch_size, wide=256):
    count, size = rows.shape
    in_vmem = pl.BlockSpec(memory_space=pltpu.VMEM)
    return pl.pallas_call(
        lambda *refs: inverse_kernel(batch_size, *refs),
        out_shape=(
            jax.ShapeDtypeStruct((count, size), f32),
            jax.ShapeDtypeStruct((2, size, own_cols), bf16),
        ),
        in_specs=[pl.BlockSpec(memory_space=pltpu.SMEM), in_vmem, in_vmem],
        out_specs=(in_vmem, in_vmem),
        scratch_shapes=[
            pltpu.VMEM((size, size), f32),
            pltpu.VMEM((size, 3 * wide), bf16),
            pltpu.VMEM((3 * wide, size), bf16),
            pltpu.VMEM((wide, size), f32),
            pltpu.VMEM((wide, wide), f32),
        ],
        compiler_params=pltpu.CompilerParams(vmem_limit_bytes=60 * 2**20),
        cost_estimate=pl.CostEstimate(
            flops=150_000_000_000, bytes_accessed=20_000_000, transcendentals=0
        ),
    )(which, packed, rows)


def sum_shares(array, axis):
    return jnp.sum(
        lax.all_to_all(array, axis, 0, 0, tiled=True).astype(f32), axis=0
    )


def three_parts(vector):
    high = lax.reduce_precision(vector, 8, 7)
    rest = vector - high
    mid = lax.reduce_precision(rest, 8, 7)
    rows = jnp.stack([high, mid, rest - mid]).astype(bf16)
    return jnp.pad(rows, ((0, 13), (0, 0)))


def body(features, proj_weight, partner):
    row_count = features.shape[0]
    feat_count = lax.axis_size("feat")
    dp_count = lax.axis_size("dp")
    own_cols = proj_weight.shape[1]
    emb_width = own_cols * feat_count
    blk_width = emb_width // (2 * feat_count)
    batch_size = row_count * dp_count
    feat_idx = lax.axis_index("feat")
    dp_idx = lax.axis_index("dp")

    def own(matrix, axis=1):
        return lax.dynamic_slice_in_dim(matrix, feat_idx * own_cols, own_cols, axis)

    def pick_cols(matrix, blk_index):
        return lax.dynamic_slice_in_dim(matrix, blk_index * blk_width, blk_width, 1)

    weight = lax.all_gather(proj_weight, "dp", axis=0, tiled=True)
    feature_sum = jnp.sum(features.astype(f32), axis=0)
    feature_sum = jnp.sum(lax.all_gather(feature_sum, "dp"), axis=0)
    feature_sum, turned = lax.optimization_barrier((feature_sum, features.T))
    col_mean = jnp.sum(mat(three_parts(feature_sum), weight), axis=0) / batch_size
    own_centered = (mat(features, weight) - col_mean).astype(bf16)
    centered = lax.all_gather(own_centered, "feat", axis=1, tiled=True)

    first = mat(pick_cols(centered, feat_idx).T, centered)
    second = mat(pick_cols(centered, 2 * feat_count - 1 - feat_idx).T, centered)
    joined = jnp.concatenate([first, second], axis=1)
    lead_cols = (feat_idx + 1) * blk_width
    shifted = lax.dynamic_slice_in_dim(joined, emb_width - lead_cols, emb_width + blk_width, 1)
    column = lax.broadcasted_iota(jnp.int32, (1, emb_width + blk_width), 1)
    cov_pack = jnp.where(column < lead_cols, joined[:, : emb_width + blk_width], shifted)
    cov_share = sum_shares(
        cov_pack.reshape(dp_count, blk_width // dp_count, emb_width + blk_width), "dp"
    )
    packed = lax.all_gather(cov_share, ("feat", "dp"), axis=0, tiled=True)
    packed = packed.reshape(feat_count, blk_width, emb_width + blk_width)

    center_sum = jnp.sum(centered.astype(f32), axis=0)
    center_sum = jnp.sum(lax.all_gather(center_sum, "dp"), axis=0)
    all_rows = jnp.concatenate([centered, three_parts(center_sum)], axis=0)
    packed, centered, all_rows = lax.optimization_barrier((packed, centered, all_rows))

    received = from_behind(centered, "dp", dp_count // 2)
    white_all, own_inverse = apply_inverse(
        packed, all_rows, feat_idx.reshape(1), own_cols, batch_size
    )
    white_rows = white_all[:row_count]
    sum_white = jnp.sum(white_all[row_count:], axis=0)
    norm_sq = jnp.sum(white_rows * centered.astype(f32), axis=1)
    local_pos = partner - (dp_idx + dp_count // 2) % dp_count * row_count
    chosen = local_pos[:, None] == lax.broadcasted_iota(jnp.int32, (row_count, row_count), 1)
    mates = mat(chosen.astype(bf16), received).astype(bf16)
    mate_sq = jnp.sum(
        jnp.where(chosen, from_behind(norm_sq, "dp", dp_count // 2)[None, :], 0.0), axis=1
    )
    mate_own = mat(mates, own_inverse[0]) + mat(mates, own_inverse[1])
    cross = jnp.sum(white_rows * mates.astype(f32), axis=1)
    inv_norm = lax.rsqrt(norm_sq + norm_eps)
    mate_inv = lax.rsqrt(mate_sq + norm_eps)
    scale = 4.0 / math.sqrt(batch_size)
    alpha = scale * inv_norm * inv_norm * (
        cross * inv_norm * mate_inv + norm_eps * inv_norm * inv_norm
    )
    beta = -scale * inv_norm * mate_inv
    own_back = alpha[:, None] * own(white_rows) + beta[:, None] * mate_own
    own_sum = jnp.sum(own_back, axis=0)

    moment = mat(centered.T, own_back.astype(bf16)) / batch_size
    shares = moment.reshape(dp_count, emb_width // dp_count, own_cols).astype(bf16)
    sum_high = lax.reduce_precision(own_sum, 8, 7)
    sum_two = jnp.stack([sum_high, own_sum - sum_high]).astype(bf16)
    sum_two = jnp.broadcast_to(jnp.pad(sum_two, ((0, 14), (0, 0))), (dp_count, 16, own_cols))
    reduced = sum_shares(jnp.concatenate([shares, sum_two], axis=1), "dp")
    own_total = reduced[-16] + reduced[-15]
    moment_share = reduced[:-16].astype(bf16)
    moment = lax.all_to_all(
        jnp.broadcast_to(moment_share, (dp_count,) + moment_share.shape), "dp", 0, 0, tiled=True
    ).reshape(emb_width, own_cols)
    back_center = own_back - mat(white_rows.astype(bf16), moment)
    sum_moment = jnp.sum(sum_white[:, None] * moment.astype(f32), axis=0)
    back_mean = (own_total - sum_moment) / batch_size
    back_proj = (back_center - back_mean).astype(bf16)
    grad = mat(turned, back_proj).astype(bf16)
    return sum_shares(grad.reshape(dp_count, -1, own_cols), "dp")


def solution(mesh):
    return jax.shard_map(
        body,
        mesh=mesh,
        in_specs=(P("dp", None), P("dp", "feat"), P("dp")),
        out_specs=P("dp", "feat"),
        check_vma=False,
    )
```

```python
import math

import jax
import jax.numpy as jnp
from jax import lax
from jax.experimental import pallas as pl
from jax.experimental.pallas import tpu as pltpu
from jax.sharding import PartitionSpec as P

ridge = 0.0001
norm_eps = 1e-06
pivot_width = 256
f32 = jnp.float32
bf16 = jnp.bfloat16


def from_behind(array, axis, by):
    peers = lax.axis_size(axis)
    return lax.ppermute(array, axis, [(i, (i + by) % peers) for i in range(peers)])


def split_two(value):
    high = value.astype(bf16)
    return high, (value - high.astype(f32)).astype(bf16)


def mat(left, right):
    return jnp.dot(left, right, preferred_element_type=f32)


def mat_fine(left, right):
    left_high, left_low = split_two(left)
    right_high, right_low = split_two(right)
    return mat(left_high, right_high) + (mat(left_high, right_low) + mat(left_low, right_high))


def invert_small(matrix, result):
    size = matrix.shape[0]
    groups = size // 8
    lane = lax.broadcasted_iota(jnp.int32, (8, size), 1)
    sub = lax.broadcasted_iota(jnp.int32, (8, size), 0)
    rows = [matrix[8 * i : 8 * i + 8] for i in range(groups)]
    for g in range(groups):
        base = 8 * g
        panel = rows[g]
        inside = (lane >= base) & (lane < base + 8)
        cols = [
            jnp.broadcast_to(panel[:, base + j : base + j + 1], (8, size)) for j in range(8)
        ]
        panel = jnp.where(inside, jnp.where(lane - base == sub, 1.0, 0.0), panel)
        for j in range(8):
            inv = 1.0 / jnp.broadcast_to(cols[j][j : j + 1, :], (8, size))
            here = sub == j
            factor = cols[j] * inv
            pivot_row = jnp.broadcast_to(panel[j : j + 1, :], (8, size))
            for m in range(j + 1, 8):
                entry = jnp.broadcast_to(cols[m][j : j + 1, :], (8, size))
                cols[m] = jnp.where(here, entry * inv, cols[m] - factor * entry)
            panel = jnp.where(here, pivot_row * inv, panel - factor * pivot_row)
        spread = [jnp.broadcast_to(panel[j : j + 1, :], (8, size)) for j in range(8)]
        for i in list(range(g + 1, groups)) + list(range(g)):
            old = rows[i]
            total = jnp.where(inside, 0.0, old)
            for j in range(8):
                total = total - (
                    jnp.broadcast_to(old[:, base + j : base + j + 1], (8, size)) * spread[j]
                )
            rows[i] = total
        rows[g] = panel
        yield
    result.append(jnp.concatenate(rows, axis=0))


def invert_panel(block, result):
    half = block.shape[0] // 2
    b11, b12 = block[:half, :half], block[:half, half:]
    b21, b22 = block[half:, :half], block[half:, half:]
    found = []
    yield from invert_small(b11, found)
    p1 = found.pop()
    r1 = mat_fine(p1, b12)
    low = mat_fine(b21, p1)
    yield from invert_small(b22 - mat_fine(b21, r1), found)
    p2 = found.pop()
    q = mat_fine(r1, p2)
    top = jnp.concatenate([p1 + mat_fine(q, low), -q], axis=1)
    bottom = jnp.concatenate([-mat_fine(p2, low), p2], axis=1)
    result.append(jnp.concatenate([top, bottom], axis=0))


def first_kernel(batch_size, total, out):
    shape = total.shape
    diagonal = lax.broadcasted_iota(jnp.int32, shape, 0) == lax.broadcasted_iota(
        jnp.int32, shape, 1
    )
    found = []
    for _ in invert_panel(total[...] * (1.0 / batch_size) + jnp.where(diagonal, ridge, 0.0), found):
        pass
    out[...] = found.pop()


def first_pivot(total, batch_size):
    return pl.pallas_call(
        lambda *refs: first_kernel(batch_size, *refs),
        out_shape=jax.ShapeDtypeStruct(total.shape, f32),
        compiler_params=pltpu.CompilerParams(vmem_limit_bytes=16 * 2**20),
    )(total)


def inverse_kernel(
    batch_size, which, packed, first, rows_in, rows_out, own_out, work, left, right, fresh, pivots
):
    pairs, blk, _ = packed.shape
    blocks = 2 * pairs
    size = work.shape[0]
    wide = fresh.shape[0]
    steps = size // wide
    diagonal = lax.broadcasted_iota(jnp.int32, (blk, blk), 0) == lax.broadcasted_iota(
        jnp.int32, (blk, blk), 1
    )
    ridge_tile = jnp.where(diagonal, ridge, 0.0)

    def unpack(a, c):
        if a < pairs:
            tile = packed[a, :, c * blk : (c + 1) * blk]
        else:
            at = (blocks - a + c) * blk
            tile = packed[blocks - 1 - a, :, at : at + blk]
        tile = tile * (1.0 / batch_size)
        if c == a:
            tile = tile + ridge_tile
        work[a * blk : (a + 1) * blk, c * blk : (c + 1) * blk] = tile
        if c != a:
            work[c * blk : (c + 1) * blk, a * blk : (a + 1) * blk] = tile.T

    tiles = [(a, c) for a in range(blocks) for c in range(a + 1)]
    for a, c in tiles:
        unpack(a, c)
    pivots[...] = first[...]

    def sweep(k, look_ahead):
        at_k = pl.ds(pl.multiple_of(k * wide, wide), wide)
        pivot = pivots[...]
        pivot_high, pivot_low = split_two(pivot)

        def scaled(lanes):
            high, low = split_two(work[at_k, lanes])
            return mat(pivot_high, high) + (mat(pivot_high, low) + mat(pivot_low, high))

        coming = []
        inversion = iter(())
        if look_ahead:
            after = pl.ds(pl.multiple_of((k + 1) * wide, wide), wide)
            row_high, row_low = split_two(scaled(after))
            col_high, col_low = split_two(work[after, at_k])
            change = mat(col_high, row_high) + (mat(col_low, row_high) + mat(col_high, row_low))
            inversion = invert_panel(work[after, after] - change, coming)
        for i in range(steps):
            rows = slice(i * wide, (i + 1) * wide)
            high, low = split_two(work[rows, at_k])
            left[rows, :wide] = high
            left[rows, wide : 2 * wide] = low
            left[rows, 2 * wide :] = high
            if i % 2 == 0:
                next(inversion, None)
        for j in range(steps):
            lanes = slice(j * wide, (j + 1) * wide)
            fresh[:, lanes] = scaled(lanes)
            if j % 2 == 0:
                next(inversion, None)
        fresh[:, at_k] = pivot
        for j in range(steps):
            lanes = slice(j * wide, (j + 1) * wide)
            high, low = split_two(fresh[:, lanes])
            right[:wide, lanes] = high
            right[wide : 2 * wide, lanes] = high
            right[2 * wide :, lanes] = low
            if j % 2 == 0:
                next(inversion, None)
        work[:, at_k] = jnp.zeros((size, wide), f32)
        for j in range(steps):
            lanes = slice(j * wide, (j + 1) * wide)
            for part in range(2):
                rows = slice(part * size // 2, (part + 1) * size // 2)
                next(inversion, None)
                if part:
                    next(inversion, None)
                work[rows, lanes] = work[rows, lanes] - mat(left[rows, :], right[:, lanes])
        for _ in inversion:
            pass
        if look_ahead:
            pivots[...] = coming.pop()
        work[at_k, :] = fresh[...]

    def step(k, carry):
        sweep(k, True)
        return carry

    lax.fori_loop(0, steps - 1, step, 0)
    sweep(steps - 1, False)

    def apply(j, carry):
        lanes = pl.ds(pl.multiple_of(j * wide, wide), wide)
        high, low = split_two(work[:, lanes])
        rows_out[:, lanes] = mat(rows_in[...], high) + mat(rows_in[...], low)
        return carry

    lax.fori_loop(0, steps, apply, 0)
    own_cols = own_out.shape[2]
    own_lanes = pl.ds(pl.multiple_of(which[0] * own_cols, own_cols), own_cols)
    high, low = split_two(work[:, own_lanes])
    own_out[0] = high
    own_out[1] = low


def apply_inverse(packed, first, rows, which, own_cols, batch_size, wide=pivot_width):
    count, size = rows.shape
    in_vmem = pl.BlockSpec(memory_space=pltpu.VMEM)
    return pl.pallas_call(
        lambda *refs: inverse_kernel(batch_size, *refs),
        out_shape=(
            jax.ShapeDtypeStruct((count, size), f32),
            jax.ShapeDtypeStruct((2, size, own_cols), bf16),
        ),
        in_specs=[pl.BlockSpec(memory_space=pltpu.SMEM), in_vmem, in_vmem, in_vmem],
        out_specs=(in_vmem, in_vmem),
        scratch_shapes=[
            pltpu.VMEM((size, size), f32),
            pltpu.VMEM((size, 3 * wide), bf16),
            pltpu.VMEM((3 * wide, size), bf16),
            pltpu.VMEM((wide, size), f32),
            pltpu.VMEM((wide, wide), f32),
        ],
        compiler_params=pltpu.CompilerParams(vmem_limit_bytes=60 * 2**20),
        cost_estimate=pl.CostEstimate(
            flops=150_000_000_000, bytes_accessed=20_000_000, transcendentals=0
        ),
    )(which, packed, first, rows)


def sum_shares(array, axis):
    return jnp.sum(
        lax.all_to_all(array, axis, 0, 0, tiled=True).astype(f32), axis=0
    )


def three_parts(vector):
    high = lax.reduce_precision(vector, 8, 7)
    rest = vector - high
    mid = lax.reduce_precision(rest, 8, 7)
    rows = jnp.stack([high, mid, rest - mid]).astype(bf16)
    return jnp.pad(rows, ((0, 13), (0, 0)))


def body(features, proj_weight, partner):
    row_count = features.shape[0]
    feat_count = lax.axis_size("feat")
    dp_count = lax.axis_size("dp")
    own_cols = proj_weight.shape[1]
    emb_width = own_cols * feat_count
    blk_width = emb_width // (2 * feat_count)
    batch_size = row_count * dp_count
    feat_idx = lax.axis_index("feat")
    dp_idx = lax.axis_index("dp")

    def own(matrix, axis=1):
        return lax.dynamic_slice_in_dim(matrix, feat_idx * own_cols, own_cols, axis)

    def pick_cols(matrix, blk_index):
        return lax.dynamic_slice_in_dim(matrix, blk_index * blk_width, blk_width, 1)

    weight = lax.all_gather(proj_weight, "dp", axis=0, tiled=True)
    feature_sum = jnp.sum(features.astype(f32), axis=0)
    feature_sum = jnp.sum(lax.all_gather(feature_sum, "dp"), axis=0)
    col_mean = jnp.sum(mat(three_parts(feature_sum), weight), axis=0) / batch_size
    own_centered = (mat(features, weight) - col_mean).astype(bf16)
    centered = lax.all_gather(own_centered, "feat", axis=1, tiled=True)

    first = mat(pick_cols(centered, feat_idx).T, centered)
    second = mat(pick_cols(centered, 2 * feat_count - 1 - feat_idx).T, centered)
    joined = jnp.concatenate([first, second], axis=1)
    lead_cols = (feat_idx + 1) * blk_width
    shifted = lax.dynamic_slice_in_dim(joined, emb_width - lead_cols, emb_width + blk_width, 1)
    column = lax.broadcasted_iota(jnp.int32, (1, emb_width + blk_width), 1)
    cov_pack = jnp.where(column < lead_cols, joined[:, : emb_width + blk_width], shifted)
    cov_share = sum_shares(
        cov_pack.reshape(dp_count, blk_width // dp_count, emb_width + blk_width), "dp"
    )
    lead = centered[:, :pivot_width]
    cov_share, lead_part = lax.optimization_barrier((cov_share, mat(lead.T, lead)))
    lead_share = sum_shares(lead_part.reshape(dp_count, -1, pivot_width), "dp")
    lead_total = lax.all_to_all(
        jnp.broadcast_to(lead_share, (dp_count,) + lead_share.shape), "dp", 0, 0, tiled=True
    ).reshape(pivot_width, pivot_width)
    first = first_pivot(lead_total, batch_size)
    packed = lax.all_gather(cov_share, ("feat", "dp"), axis=0, tiled=True)
    packed = packed.reshape(feat_count, blk_width, emb_width + blk_width)

    center_sum = jnp.sum(centered.astype(f32), axis=0)
    center_sum = jnp.sum(lax.all_gather(center_sum, "dp"), axis=0)
    all_rows = jnp.concatenate([centered, three_parts(center_sum)], axis=0)
    packed, first, centered, all_rows = lax.optimization_barrier(
        (packed, first, centered, all_rows)
    )

    received = from_behind(centered, "dp", dp_count // 2)
    white_all, own_inverse = apply_inverse(
        packed, first, all_rows, feat_idx.reshape(1), own_cols, batch_size
    )
    white_rows = white_all[:row_count]
    sum_white = jnp.sum(white_all[row_count:], axis=0)
    norm_sq = jnp.sum(white_rows * centered.astype(f32), axis=1)
    local_pos = partner - (dp_idx + dp_count // 2) % dp_count * row_count
    chosen = local_pos[:, None] == lax.broadcasted_iota(jnp.int32, (row_count, row_count), 1)
    mates = mat(chosen.astype(bf16), received).astype(bf16)
    mate_sq = jnp.sum(
        jnp.where(chosen, from_behind(norm_sq, "dp", dp_count // 2)[None, :], 0.0), axis=1
    )
    mate_own = mat(mates, own_inverse[0]) + mat(mates, own_inverse[1])
    cross = jnp.sum(white_rows * mates.astype(f32), axis=1)
    inv_norm = lax.rsqrt(norm_sq + norm_eps)
    mate_inv = lax.rsqrt(mate_sq + norm_eps)
    scale = 4.0 / math.sqrt(batch_size)
    alpha = scale * inv_norm * inv_norm * (
        cross * inv_norm * mate_inv + norm_eps * inv_norm * inv_norm
    )
    beta = -scale * inv_norm * mate_inv
    own_back = alpha[:, None] * own(white_rows) + beta[:, None] * mate_own
    own_sum = jnp.sum(own_back, axis=0)

    moment = mat(centered.T, own_back.astype(bf16)) / batch_size
    shares = moment.reshape(dp_count, emb_width // dp_count, own_cols).astype(bf16)
    sum_high = lax.reduce_precision(own_sum, 8, 7)
    sum_two = jnp.stack([sum_high, own_sum - sum_high]).astype(bf16)
    sum_two = jnp.broadcast_to(jnp.pad(sum_two, ((0, 14), (0, 0))), (dp_count, 16, own_cols))
    reduced = sum_shares(jnp.concatenate([shares, sum_two], axis=1), "dp")
    own_total = reduced[-16] + reduced[-15]
    moment_share = reduced[:-16].astype(bf16)
    moment = lax.all_to_all(
        jnp.broadcast_to(moment_share, (dp_count,) + moment_share.shape), "dp", 0, 0, tiled=True
    ).reshape(emb_width, own_cols)
    back_center = own_back - mat(white_rows.astype(bf16), moment)
    sum_moment = jnp.sum(sum_white[:, None] * moment.astype(f32), axis=0)
    back_mean = (own_total - sum_moment) / batch_size
    back_proj = (back_center - back_mean).astype(bf16)
    grad = mat(features.T, back_proj).astype(bf16)
    return sum_shares(grad.reshape(dp_count, -1, own_cols), "dp")


def solution(mesh):
    return jax.shard_map(
        body,
        mesh=mesh,
        in_specs=(P("dp", None), P("dp", "feat"), P("dp")),
        out_specs=P("dp", "feat"),
        check_vma=False,
    )
```

```python
import math

import jax
import jax.numpy as jnp
from jax import lax
from jax.experimental.layout import Layout, with_layout_constraint
from jax.experimental import pallas as pl
from jax.experimental.pallas import tpu as pltpu
from jax.sharding import PartitionSpec as P

ridge = 0.0001
norm_eps = 1e-06
pivot_width = 256
f32 = jnp.float32
bf16 = jnp.bfloat16


def from_behind(array, axis, by):
    peers = lax.axis_size(axis)
    return lax.ppermute(array, axis, [(i, (i + by) % peers) for i in range(peers)])


def split_two(value):
    high = value.astype(bf16)
    return high, (value - high.astype(f32)).astype(bf16)


def mat(left, right):
    return jnp.dot(left, right, preferred_element_type=f32)


def mat_fine(left, right):
    left_high, left_low = split_two(left)
    right_high, right_low = split_two(right)
    return mat(left_high, right_high) + (mat(left_high, right_low) + mat(left_low, right_high))


def invert_small(matrix, result):
    size = matrix.shape[0]
    groups = size // 8
    lane = lax.broadcasted_iota(jnp.int32, (8, size), 1)
    sub = lax.broadcasted_iota(jnp.int32, (8, size), 0)
    rows = [matrix[8 * i : 8 * i + 8] for i in range(groups)]
    for g in range(groups):
        base = 8 * g
        panel = rows[g]
        inside = (lane >= base) & (lane < base + 8)
        cols = [
            jnp.broadcast_to(panel[:, base + j : base + j + 1], (8, size)) for j in range(8)
        ]
        panel = jnp.where(inside, jnp.where(lane - base == sub, 1.0, 0.0), panel)
        for j in range(8):
            inv = 1.0 / jnp.broadcast_to(cols[j][j : j + 1, :], (8, size))
            here = sub == j
            factor = cols[j] * inv
            pivot_row = jnp.broadcast_to(panel[j : j + 1, :], (8, size))
            for m in range(j + 1, 8):
                entry = jnp.broadcast_to(cols[m][j : j + 1, :], (8, size))
                cols[m] = jnp.where(here, entry * inv, cols[m] - factor * entry)
            panel = jnp.where(here, pivot_row * inv, panel - factor * pivot_row)
        spread = [jnp.broadcast_to(panel[j : j + 1, :], (8, size)) for j in range(8)]
        for i in list(range(g + 1, groups)) + list(range(g)):
            old = rows[i]
            total = jnp.where(inside, 0.0, old)
            for j in range(8):
                total = total - (
                    jnp.broadcast_to(old[:, base + j : base + j + 1], (8, size)) * spread[j]
                )
            rows[i] = total
        rows[g] = panel
        yield
    result.append(jnp.concatenate(rows, axis=0))


def invert_panel(block, result):
    half = block.shape[0] // 2
    b11, b12 = block[:half, :half], block[:half, half:]
    b21, b22 = block[half:, :half], block[half:, half:]
    found = []
    yield from invert_small(b11, found)
    p1 = found.pop()
    r1 = mat_fine(p1, b12)
    low = mat_fine(b21, p1)
    yield from invert_small(b22 - mat_fine(b21, r1), found)
    p2 = found.pop()
    q = mat_fine(r1, p2)
    top = jnp.concatenate([p1 + mat_fine(q, low), -q], axis=1)
    bottom = jnp.concatenate([-mat_fine(p2, low), p2], axis=1)
    result.append(jnp.concatenate([top, bottom], axis=0))


def first_kernel(batch_size, total, out):
    shape = total.shape
    diagonal = lax.broadcasted_iota(jnp.int32, shape, 0) == lax.broadcasted_iota(
        jnp.int32, shape, 1
    )
    found = []
    for _ in invert_panel(total[...] * (1.0 / batch_size) + jnp.where(diagonal, ridge, 0.0), found):
        pass
    out[...] = found.pop()


def first_pivot(total, batch_size):
    return pl.pallas_call(
        lambda *refs: first_kernel(batch_size, *refs),
        out_shape=jax.ShapeDtypeStruct(total.shape, f32),
        compiler_params=pltpu.CompilerParams(vmem_limit_bytes=16 * 2**20),
    )(total)


def inverse_kernel(
    batch_size, which, packed, first, rows_in, rows_out, own_out, work, left, right, fresh, pivots
):
    pairs, blk, _ = packed.shape
    blocks = 2 * pairs
    size = work.shape[0]
    wide = fresh.shape[0]
    steps = size // wide
    diagonal = lax.broadcasted_iota(jnp.int32, (blk, blk), 0) == lax.broadcasted_iota(
        jnp.int32, (blk, blk), 1
    )
    ridge_tile = jnp.where(diagonal, ridge, 0.0)

    def unpack(a, c):
        if a < pairs:
            tile = packed[a, :, c * blk : (c + 1) * blk]
        else:
            at = (blocks - a + c) * blk
            tile = packed[blocks - 1 - a, :, at : at + blk]
        tile = tile * (1.0 / batch_size)
        if c == a:
            tile = tile + ridge_tile
        work[a * blk : (a + 1) * blk, c * blk : (c + 1) * blk] = tile
        if c != a:
            work[c * blk : (c + 1) * blk, a * blk : (a + 1) * blk] = tile.T

    tiles = [(a, c) for a in range(blocks) for c in range(a + 1)]
    for a, c in tiles:
        unpack(a, c)
    pivots[...] = first[...]

    def sweep(k, look_ahead):
        at_k = pl.ds(pl.multiple_of(k * wide, wide), wide)
        pivot = pivots[...]
        pivot_high, pivot_low = split_two(pivot)

        def scaled(lanes):
            high, low = split_two(work[at_k, lanes])
            return mat(pivot_high, high) + (mat(pivot_high, low) + mat(pivot_low, high))

        coming = []
        inversion = iter(())
        if look_ahead:
            after = pl.ds(pl.multiple_of((k + 1) * wide, wide), wide)
            row_high, row_low = split_two(scaled(after))
            col_high, col_low = split_two(work[after, at_k])
            change = mat(col_high, row_high) + (mat(col_low, row_high) + mat(col_high, row_low))
            inversion = invert_panel(work[after, after] - change, coming)
        for i in range(steps):
            rows = slice(i * wide, (i + 1) * wide)
            high, low = split_two(work[rows, at_k])
            left[rows, :wide] = high
            left[rows, wide : 2 * wide] = low
            left[rows, 2 * wide :] = high
            if i % 2 == 0:
                next(inversion, None)
        for j in range(steps):
            lanes = slice(j * wide, (j + 1) * wide)
            fresh[:, lanes] = scaled(lanes)
            if j % 2 == 0:
                next(inversion, None)
        fresh[:, at_k] = pivot
        for j in range(steps):
            lanes = slice(j * wide, (j + 1) * wide)
            high, low = split_two(fresh[:, lanes])
            right[:wide, lanes] = high
            right[wide : 2 * wide, lanes] = high
            right[2 * wide :, lanes] = low
            if j % 2 == 0:
                next(inversion, None)
        work[:, at_k] = jnp.zeros((size, wide), f32)
        for j in range(steps):
            lanes = slice(j * wide, (j + 1) * wide)
            for part in range(2):
                rows = slice(part * size // 2, (part + 1) * size // 2)
                next(inversion, None)
                if part:
                    next(inversion, None)
                work[rows, lanes] = work[rows, lanes] - mat(left[rows, :], right[:, lanes])
        for _ in inversion:
            pass
        if look_ahead:
            pivots[...] = coming.pop()
        work[at_k, :] = fresh[...]

    def step(k, carry):
        sweep(k, True)
        return carry

    lax.fori_loop(0, steps - 1, step, 0)
    sweep(steps - 1, False)

    def apply(j, carry):
        lanes = pl.ds(pl.multiple_of(j * wide, wide), wide)
        high, low = split_two(work[:, lanes])
        rows_out[:, lanes] = mat(rows_in[...], high) + mat(rows_in[...], low)
        return carry

    lax.fori_loop(0, steps, apply, 0)
    own_cols = own_out.shape[2]
    own_lanes = pl.ds(pl.multiple_of(which[0] * own_cols, own_cols), own_cols)
    high, low = split_two(work[:, own_lanes])
    own_out[0] = high
    own_out[1] = low


def apply_inverse(packed, first, rows, which, own_cols, batch_size, wide=pivot_width):
    count, size = rows.shape
    in_vmem = pl.BlockSpec(memory_space=pltpu.VMEM)
    return pl.pallas_call(
        lambda *refs: inverse_kernel(batch_size, *refs),
        out_shape=(
            jax.ShapeDtypeStruct((count, size), f32),
            jax.ShapeDtypeStruct((2, size, own_cols), bf16),
        ),
        in_specs=[pl.BlockSpec(memory_space=pltpu.SMEM), in_vmem, in_vmem, in_vmem],
        out_specs=(in_vmem, in_vmem),
        scratch_shapes=[
            pltpu.VMEM((size, size), f32),
            pltpu.VMEM((size, 3 * wide), bf16),
            pltpu.VMEM((3 * wide, size), bf16),
            pltpu.VMEM((wide, size), f32),
            pltpu.VMEM((wide, wide), f32),
        ],
        compiler_params=pltpu.CompilerParams(vmem_limit_bytes=60 * 2**20),
        cost_estimate=pl.CostEstimate(
            flops=150_000_000_000, bytes_accessed=20_000_000, transcendentals=0
        ),
    )(which, packed, first, rows)


def sum_shares(array, axis):
    return jnp.sum(
        lax.all_to_all(array, axis, 0, 0, tiled=True).astype(f32), axis=0
    )


def three_parts(vector):
    high = lax.reduce_precision(vector, 8, 7)
    rest = vector - high
    mid = lax.reduce_precision(rest, 8, 7)
    rows = jnp.stack([high, mid, rest - mid]).astype(bf16)
    return jnp.pad(rows, ((0, 13), (0, 0)))


def body(features, proj_weight, partner):
    row_count = features.shape[0]
    feat_count = lax.axis_size("feat")
    dp_count = lax.axis_size("dp")
    own_cols = proj_weight.shape[1]
    emb_width = own_cols * feat_count
    blk_width = emb_width // (2 * feat_count)
    batch_size = row_count * dp_count
    feat_idx = lax.axis_index("feat")
    dp_idx = lax.axis_index("dp")

    def own(matrix, axis=1):
        return lax.dynamic_slice_in_dim(matrix, feat_idx * own_cols, own_cols, axis)

    def pick_cols(matrix, blk_index):
        return lax.dynamic_slice_in_dim(matrix, blk_index * blk_width, blk_width, 1)

    weight = lax.all_gather(proj_weight, "dp", axis=0, tiled=True)
    feature_sum = jnp.sum(features.astype(f32), axis=0)
    feature_sum = jnp.sum(lax.all_gather(feature_sum, "dp"), axis=0)
    turned = with_layout_constraint(features.T, Layout(major_to_minor=(0, 1)))
    sum_parts, turned = lax.optimization_barrier((three_parts(feature_sum), turned))
    col_mean = jnp.sum(mat(sum_parts, weight), axis=0) / batch_size
    own_centered = (mat(features, weight) - col_mean).astype(bf16)
    centered = lax.all_gather(own_centered, "feat", axis=1, tiled=True)

    first = mat(pick_cols(centered, feat_idx).T, centered)
    second = mat(pick_cols(centered, 2 * feat_count - 1 - feat_idx).T, centered)
    joined = jnp.concatenate([first, second], axis=1)
    lead_cols = (feat_idx + 1) * blk_width
    shifted = lax.dynamic_slice_in_dim(joined, emb_width - lead_cols, emb_width + blk_width, 1)
    column = lax.broadcasted_iota(jnp.int32, (1, emb_width + blk_width), 1)
    cov_pack = jnp.where(column < lead_cols, joined[:, : emb_width + blk_width], shifted)
    cov_share = sum_shares(
        cov_pack.reshape(dp_count, blk_width // dp_count, emb_width + blk_width), "dp"
    )
    lead = centered[:, :pivot_width]
    cov_share, lead_part = lax.optimization_barrier((cov_share, mat(lead.T, lead)))
    lead_share = sum_shares(lead_part.reshape(dp_count, -1, pivot_width), "dp")
    lead_total = lax.all_to_all(
        jnp.broadcast_to(lead_share, (dp_count,) + lead_share.shape), "dp", 0, 0, tiled=True
    ).reshape(pivot_width, pivot_width)
    first = first_pivot(lead_total, batch_size)
    packed = lax.all_gather(cov_share, ("feat", "dp"), axis=0, tiled=True)
    packed = packed.reshape(feat_count, blk_width, emb_width + blk_width)

    center_sum = jnp.sum(centered.astype(f32), axis=0)
    center_sum = jnp.sum(lax.all_gather(center_sum, "dp"), axis=0)
    all_rows = jnp.concatenate([centered, three_parts(center_sum)], axis=0)
    packed, first, centered, all_rows = lax.optimization_barrier(
        (packed, first, centered, all_rows)
    )

    received = from_behind(centered, "dp", dp_count // 2)
    white_all, own_inverse = apply_inverse(
        packed, first, all_rows, feat_idx.reshape(1), own_cols, batch_size
    )
    white_rows = white_all[:row_count]
    sum_white = jnp.sum(white_all[row_count:], axis=0)
    norm_sq = jnp.sum(white_rows * centered.astype(f32), axis=1)
    local_pos = partner - (dp_idx + dp_count // 2) % dp_count * row_count
    chosen = local_pos[:, None] == lax.broadcasted_iota(jnp.int32, (row_count, row_count), 1)
    mates = mat(chosen.astype(bf16), received).astype(bf16)
    mate_sq = jnp.sum(
        jnp.where(chosen, from_behind(norm_sq, "dp", dp_count // 2)[None, :], 0.0), axis=1
    )
    mate_own = mat(mates, own_inverse[0]) + mat(mates, own_inverse[1])
    cross = jnp.sum(white_rows * mates.astype(f32), axis=1)
    inv_norm = lax.rsqrt(norm_sq + norm_eps)
    mate_inv = lax.rsqrt(mate_sq + norm_eps)
    scale = 4.0 / math.sqrt(batch_size)
    alpha = scale * inv_norm * inv_norm * (
        cross * inv_norm * mate_inv + norm_eps * inv_norm * inv_norm
    )
    beta = -scale * inv_norm * mate_inv
    own_back = alpha[:, None] * own(white_rows) + beta[:, None] * mate_own
    own_sum = jnp.sum(own_back, axis=0)

    moment = mat(centered.T, own_back.astype(bf16)) / batch_size
    shares = moment.reshape(dp_count, emb_width // dp_count, own_cols).astype(bf16)
    sum_high = lax.reduce_precision(own_sum, 8, 7)
    sum_two = jnp.stack([sum_high, own_sum - sum_high]).astype(bf16)
    sum_two = jnp.broadcast_to(jnp.pad(sum_two, ((0, 14), (0, 0))), (dp_count, 16, own_cols))
    reduced = sum_shares(jnp.concatenate([shares, sum_two], axis=1), "dp")
    own_total = reduced[-16] + reduced[-15]
    moment_share = reduced[:-16].astype(bf16)
    moment = lax.all_to_all(
        jnp.broadcast_to(moment_share, (dp_count,) + moment_share.shape), "dp", 0, 0, tiled=True
    ).reshape(emb_width, own_cols)
    back_center = own_back - mat(white_rows.astype(bf16), moment)
    sum_moment = jnp.sum(sum_white[:, None] * moment.astype(f32), axis=0)
    back_mean = (own_total - sum_moment) / batch_size
    back_proj = (back_center - back_mean).astype(bf16)
    grad = mat(turned, back_proj).astype(bf16)
    return sum_shares(grad.reshape(dp_count, -1, own_cols), "dp")


def solution(mesh):
    return jax.shard_map(
        body,
        mesh=mesh,
        in_specs=(P("dp", None), P("dp", "feat"), P("dp")),
        out_specs=P("dp", "feat"),
        check_vma=False,
    )
```
